256 devices in a mesh: dp: 8 (over y, core), tensor: 32 (over x, z).
Axes of the slice: x: 4, y: 4, z: 8, core: 2. Of those that a mesh axis runs over, the one named last changes fastest.
Arguments:
- act: bfloat16 [2048, 5120], P(None, 'dp'), may hold values from -6 to 6
- cot: bfloat16 [2048, 25600], P('dp', 'tensor'), may hold values from -0.3125 to 0.3125
- momentum: float32 [5120, 25600], P('dp', 'tensor'), may hold values from -150 to 150
Outputs:
- new_momentum: float32 [5120, 25600], P('dp', 'tensor')
- update: bfloat16 [5120, 25600], P('dp', 'tensor')
The draws below stay inside these ranges and needn't reach their ends.
All inputs are finite; a program needn't handle non-finite values.
Results may differ from the reference program's by a relative error of at most 0.02.
Values may be sent and summed in bfloat16 or wider, within the bound.
A program may use at most 128 MiB of HBM per device.

```python
import jax
import jax.numpy as jnp
from jax import lax

D = 5120
FF = 25600
TOKENS = 2048
N_TENSOR = 32


def draw_momentum(key, part):
    key = jax.random.fold_in(key, 11)
    key_base, key_rows, key_cols = jax.random.split(key, 3)
    base = jnp.clip(jax.random.normal(key_base, (D, FF), jnp.float32), -4.0, 4.0)
    top = 2.0
    rising_rows = jnp.arange(D, dtype=jnp.float32)[:, None] / D
    rising_cols = jnp.arange(FF, dtype=jnp.float32)[None, :] / FF
    row_scale = jnp.exp(jnp.log(3.0) * rising_rows + jnp.log(top) * jax.random.uniform(key_rows, (D, 1), jnp.float32))
    col_scale = jnp.exp(jnp.log(3.0) * rising_cols + jnp.log(top) * jax.random.uniform(key_cols, (1, FF), jnp.float32))
    return base * row_scale * col_scale


def levels(own_key, shape, shards, smallest, top_value):
    factor_of, own = 1.0, jax.random.fold_in(own_key, 6)
    for position, shards_of in shards:
        heights = jnp.exp(jax.random.uniform(jax.random.fold_in(own, position), (shards_of,), jnp.float32, smallest / len(shards), top_value / len(shards)))
        factor_of = factor_of * jnp.repeat(heights, shape[position] // shards_of).reshape([-1 if axis == position else 1 for axis in range(len(shape))])
    return factor_of


def gaussian(stream_key, dims, scale, limit, cuts=(), kind=jnp.bfloat16):
    values = scale * jax.random.normal(stream_key, dims, jnp.float32)
    if cuts:
        values = values * levels(stream_key, dims, cuts, -0.22, 0.18)
    return jnp.clip(values, -limit, limit).astype(kind)


def setup_inputs(seed: int = 0) -> dict:
    keys = jax.random.split(jax.random.key(seed), 4)
    return {
        "act": gaussian(keys[0], (TOKENS, D), 1.0, 6.0, ((1, 8),)),
        "cot": gaussian(keys[1], (TOKENS, FF), (TOKENS ** -0.5), 0.3125, ((0, 8), (1, 32))),
        "momentum": draw_momentum(jax.random.fold_in(keys[3], 71), 0),
    }


def gram_of(ortho):
    width = FF // N_TENSOR
    blocks = ortho.reshape(D, N_TENSOR, width).transpose(1, 0, 2)

    def add_block(total, block):
        part = jnp.dot(block, block.T, preferred_element_type=jnp.float32).astype(jnp.bfloat16)
        part = lax.optimization_barrier(part)
        return (total + part.astype(jnp.float32), None)
    summed, _ = lax.scan(add_block, jnp.zeros((D, D), jnp.float32), blocks)
    return summed.astype(jnp.bfloat16)

def reference(act, cot, momentum):
    grad = jnp.dot(act.T, cot, preferred_element_type=jnp.float32)
    new_momentum = 0.95 * momentum + grad
    nesterov = grad + 0.95 * new_momentum
    total = jnp.sum(nesterov * nesterov)
    factor = 0.55 * jnp.sqrt(jnp.float32(D)) / jnp.sqrt(total + 1e-06)
    ortho = (nesterov * factor).astype(jnp.bfloat16)
    gram = gram_of(ortho)
    square = jnp.dot(gram, gram, preferred_element_type=jnp.float32)
    mix = (-4.775 * gram.astype(jnp.float32) + 2.0315 * square).astype(jnp.bfloat16)
    spread = jnp.dot(mix, ortho, preferred_element_type=jnp.float32)
    scale = 0.2 * max(D, FF) ** 0.5
    update = (scale * (3.4445 * ortho.astype(jnp.float32) + spread)).astype(jnp.bfloat16)
    return (new_momentum, update)
```

```python
import functools

import jax
import jax.numpy as jnp
from jax import lax
from jax.experimental import pallas as pl
from jax.experimental.pallas import tpu as pltpu
from jax.sharding import PartitionSpec as P

D = 5120
FF = 25600
NY, NX, NZ = 4, 4, 8
ROWS, COLS = 640, 800
TOK = 256
UNITS, PIECE = 10, 16
MESH = pl.DeviceIdType.MESH
BF, F32 = jnp.bfloat16, jnp.float32


class Place:
    def __init__(self):
        self.dp, self.tensor = lax.axis_index("dp"), lax.axis_index("tensor")
        self.y, self.core = self.dp // 2, self.dp % 2
        self.x, self.z = self.tensor // NZ, self.tensor % NZ

    def to_y(self, step):
        return (lax.rem(self.y + step + NY, NY) * 2 + self.core, self.tensor)

    def to_x(self, step):
        return (self.dp, lax.rem(self.x + step + NX, NX) * NZ + self.z)

    def to_z(self, step):
        return (self.dp, self.x * NZ + lax.rem(self.z + step + NZ, NZ))

    def sibling(self):
        return (self.y * 2 + 1 - self.core, self.tensor)


def send(src, dst, send_sem, recv_sem, device):
    copy = pltpu.make_async_remote_copy(
        src_ref=src, dst_ref=dst, send_sem=send_sem, recv_sem=recv_sem,
        device_id=device, device_id_type=MESH,
    )
    copy.start()


def wait(ref, sem):
    pltpu.make_async_copy(ref, ref, sem).wait()


def greet(devices):
    barrier = pltpu.get_barrier_semaphore()
    for device in devices:
        pl.semaphore_signal(barrier, inc=1, device_id=device, device_id_type=MESH)
    pl.semaphore_wait(barrier, len(devices))


def dot(a, b, ca, cb):
    return lax.dot_general(a, b, (((ca,), (cb,)), ((), ())), preferred_element_type=F32)


class Sum:
    def __init__(self, n1, n2, p1, p2, to1, to2, part, got, full, ss, rs):
        self.n1, self.n2, self.p1 = n1, n2, p1
        self.part, self.got, self.full, self.ss, self.rs = part, got, full, ss, rs
        self.h1, self.h2 = h1, h2 = n1 // 2, n2 // 2
        self.dev1 = {sign: to1(sign) for sign in (1, -1)}
        self.dev2 = {sign: to2(sign) for sign in (1, -1)}
        self.at1 = {d: lax.rem(p1 + d + n1, n1) * n2 for d in range(-h1, h1 + 1)}
        self.at2 = {d: p1 * n2 + lax.rem(p2 + d + n2, n2) for d in range(-h2, h2 + 1)}
        self.msg, offset = {}, 0
        for stage in range(2 * h1 + 2 * h2):
            for role in (0, 1):
                kind, length = self.kind(stage, role)
                if kind is not None:
                    self.msg[stage, role] = (length, offset)
                    offset += length if stage < h1 + h2 else 0

    def kind(self, stage, role):
        h1, h2, n2 = self.h1, self.h2, self.n2
        if stage < h1:
            return "rs1", n2 // 2 if stage == 0 else n2
        if stage < h1 + h2:
            return ("rs2" if stage > h1 or role == 0 else None), 1
        if stage < h1 + 2 * h2:
            last = stage == h1 + 2 * h2 - 1
            return (None if last and role == 1 else "ag2"), 1
        last = stage == 2 * h1 + 2 * h2 - 1
        return "ag1", n2 // 2 if last else n2

    def second(self, role, unit, table, d=1):
        upward = lax.rem(unit, 2) == role
        pick = lambda a, b: jnp.where(upward, a, b)
        a, b = table[d], table[-d]
        return tuple(map(pick, a, b)) if isinstance(a, tuple) else pick(a, b)

    def launch(self, stage, role, unit, src, dst):
        first = stage < self.h1 or stage >= self.h1 + 2 * self.h2
        to = self.dev1[1 - 2 * role] if first else self.second(role, unit, self.dev2)
        send(src, dst, self.ss.at[unit], self.rs.at[unit, stage], to)

    def slab(self, stage, role, unit):
        length, offset = self.msg[stage, role]
        return self.got.at[unit, pl.ds(offset, length)]

    def add(self, unit, at, length, *slabs, out=None):
        total = self.part[unit, pl.ds(at, length)].astype(F32)
        for slab in slabs:
            total = total + slab[...].astype(F32)
        if out is None:
            self.part[unit, pl.ds(at, length)] = total.astype(BF)
        else:
            out[unit, pl.ds(at, length)] = total.astype(BF)

    def settle(self, stage, unit):
        total = sum(self.msg[stage, role][0] for role in (0, 1) if (stage, role) in self.msg)
        wait(self.part.at[unit, pl.ds(0, total)], self.rs.at[unit, stage])

    def run(self, stage, unit):
        h1, h2, n2 = self.h1, self.h2, self.n2
        part, full = self.part, self.full
        if stage > 0:
            self.settle(stage - 1, unit)
        if stage < h1:
            step = h1 - stage
            for role in (0, 1):
                sign = 1 - 2 * role
                if stage == 0:
                    at = self.at1[h1] + role * (n2 // 2)
                else:
                    at = self.at1[sign * step]
                    if stage == 1:
                        self.add(unit, at + role * (n2 // 2), n2 // 2, self.slab(0, role, unit))
                    else:
                        self.add(unit, at, n2, self.slab(stage - 1, role, unit))
                length = self.msg[stage, role][0]
                self.launch(stage, role, unit, part.at[unit, pl.ds(at, length)],
                            self.slab(stage, role, unit))
        elif stage < h1 + h2:
            if stage == h1:
                own = self.p1 * n2
                self.add(unit, own, n2, self.slab(stage - 1, 0, unit), self.slab(stage - 1, 1, unit))
            step = h1 + h2 - stage
            for role in (0, 1):
                if (stage, role) not in self.msg:
                    continue
                at = self.second(role, unit, self.at2, step)
                if stage > h1 and (stage - 1, role) in self.msg:
                    self.add(unit, at, 1, self.slab(stage - 1, role, unit))
                self.launch(stage, role, unit, part.at[unit, pl.ds(at, 1)],
                            self.slab(stage, role, unit))
        elif stage < h1 + 2 * h2:
            at = self.at2[0]
            hop = stage - h1 - h2
            if hop == 0:
                self.add(unit, at, 1, self.slab(stage - 1, 0, unit), self.slab(stage - 1, 1, unit),
                         out=full)
            for role in (0, 1):
                if (stage, role) in self.msg:
                    at = self.second(1 - role, unit, self.at2, hop)
                    piece = full.at[unit, pl.ds(at, 1)]
                    self.launch(stage, role, unit, piece, piece)
        elif stage < 2 * h1 + 2 * h2:
            hop = stage - h1 - 2 * h2
            for role in (0, 1):
                sign = 1 - 2 * role
                at = self.at1[-sign * hop]
                length = self.msg[stage, role][0]
                if length < n2:
                    at = at + role * (n2 // 2)
                piece = full.at[unit, pl.ds(at, length)]
                self.launch(stage, role, unit, piece, piece)


STAGES = 12
SKEW = 3
SPACE = 2
START = 22
FORWARD = 12
GROUPS = ((0, 256), (256, 256), (512, 128))


def unit_at(k):
    return jnp.where(k == 1, 4, jnp.where(jnp.logical_and(k >= 2, k < 5), k - 1, jnp.where(k == 0, 0, k)))


def entry(k):
    return k if k < 2 else START + SPACE * (k - 2)


def kernel(act_hbm, cot, mom_hbm, newm, update, act, held, cols, ours, theirs, twin,
           part, got, full, spread, acc, away, came, tot,
           ls, cs, cr, ns, nr, ss, rs, ps, pr, xs, xr, ts, tr):
    me = Place()
    up, down, sib = me.to_y(1), me.to_y(-1), me.sibling()
    load_act = pltpu.make_async_copy(act_hbm, act, ls.at[0])
    load_mom = pltpu.make_async_copy(mom_hbm, newm, ls.at[1])
    load_act.start()
    load_mom.start()
    greet([up, down, sib, me.to_x(1), me.to_x(-1), me.to_z(1), me.to_z(-1)])

    half = COLS // 2
    other = 1 - me.core

    def block(step, core):
        return lax.rem(me.y + step + NY, NY) * 2 + core

    def bit(step, core, h):
        return held.at[block(step, core), pl.ds(h * half, half)]

    own0, own1 = cot.at[pl.ds(0, half)], cot.at[pl.ds(half, half)]
    send(own0, bit(0, me.core, 0), cs.at[0], cr.at[0], up)
    send(own1, bit(0, me.core, 1), cs.at[1], cr.at[1], down)
    send(cot, held.at[me.dp], cs.at[2], cr.at[2], sib)
    send(own1, bit(0, me.core, 1), cs.at[3], cr.at[3], up)
    send(own0, bit(0, me.core, 0), cs.at[4], cr.at[4], down)
    load_act.wait()

    def term(tokens, rows):
        return dot(rows, act[pl.ds(pl.multiple_of(tokens * TOK, TOK), TOK), :], 1, 0)

    acc[0] = term(me.dp, cot[...])
    wait(own0, cr.at[0])
    send(bit(-1, me.core, 0), bit(-1, me.core, 0), cs.at[5], cr.at[5], up)
    wait(own1, cr.at[1])
    send(bit(1, me.core, 1), bit(1, me.core, 1), cs.at[6], cr.at[6], down)
    wait(cot, cr.at[2])
    acc[0] += term(block(0, other), held[block(0, other)])
    low, high = held.at[block(-1, me.core)], held.at[block(1, me.core)]
    wait(own1, cr.at[3])
    send(low, low, cs.at[7], cr.at[7], sib)
    wait(own0, cr.at[4])
    send(high, high, cs.at[8], cr.at[8], sib)
    acc[0] += term(block(-1, me.core), low[...])
    acc[0] += term(block(1, me.core), high[...])
    wait(low, cr.at[7])
    acc[0] += term(block(-1, other), held[block(-1, other)])
    wait(high, cr.at[8])
    acc[0] += term(block(1, other), held[block(1, other)])
    wait(own0, cr.at[5])
    send(bit(2, me.core, 0), bit(2, me.core, 0), cs.at[9], cr.at[9], sib)
    wait(own1, cr.at[6])
    send(bit(2, me.core, 1), bit(2, me.core, 1), cs.at[10], cr.at[10], sib)
    acc[0] += term(block(2, me.core), held[block(2, me.core)])
    wait(own0, cr.at[9])
    wait(own1, cr.at[10])
    acc[0] += term(block(2, other), held[block(2, other)])
    load_mom.wait()

    strip = 80

    def momentum(i, squares):
        rows = pl.ds(pl.multiple_of(i * strip, strip), strip)
        grad = acc[0, rows]
        updated = 0.95 * newm[rows] + grad
        newm[rows] = updated
        value = grad + 0.95 * updated
        cols[0, rows] = value.astype(BF)
        return squares + jnp.sum(value * value, axis=0, keepdims=True)

    squares = lax.fori_loop(0, COLS // strip, momentum, jnp.zeros((1, ROWS), F32))
    tot[0] = jnp.full((8, 128), jnp.sum(squares), F32)

    def slot(s, h):
        return cols.at[s, pl.ds(h * half, half)]

    send(cols.at[0], twin, ns.at[0], nr.at[0], sib)
    send(slot(0, 0), slot(2, 0), ns.at[1], nr.at[1], up)
    send(slot(0, 1), slot(1, 1), ns.at[2], nr.at[2], down)
    send(slot(0, 1), slot(2, 1), ns.at[3], nr.at[3], up)
    send(slot(0, 0), slot(1, 0), ns.at[4], nr.at[4], down)
    ours[...] = cols[0].T
    wait(twin, nr.at[0])
    theirs[...] = twin[...].T

    sums = (
        Sum(NX, NZ, me.x, me.z, me.to_x, me.to_z, part, got, full, ss, rs),
        Sum(NZ, NX, me.z, me.x, me.to_z, me.to_x, part, got, full, ss, rs),
    )

    def gram(unit):
        def put(at, chip_rows, length, s):
            value = dot(chip_rows, cols[s], 1, 0).astype(BF)
            part[unit, pl.ds(at, length // PIECE)] = value.reshape(length // PIECE, PIECE, ROWS)

        def from_cores(at0, at1, first, length, s):
            put(jnp.where(me.core == 0, at0, at1), ours[pl.ds(first, length), :], length, s)
            put(jnp.where(me.core == 0, at1, at0), theirs[pl.ds(first, length), :], length, s)

        @pl.when(unit < 8)
        def _():
            first = pl.multiple_of((unit // 4) * 256, 256)
            from_cores(0, 16, first, 256, lax.rem(unit, 4))

        @pl.when(unit >= 8)
        def _():
            for k in (0, 1):
                from_cores(16 * k, 16 * k + 8, 512, 128, (unit - 8) * 2 + k)

    def rider(k):
        def go(src, dst, index, device):
            send(tot.at[src], tot.at[dst], ts.at[index], tr.at[dst], device)

        def here(*slots):
            for s in slots:
                wait(tot.at[s], tr.at[s])

        def put(dst, first, last):
            value = tot[first]
            for s in range(first + 1, last):
                value = value + tot[s]
            tot[dst] = value

        if k == 0:
            go(0, 1, 0, me.to_x(1))
            go(0, 2, 1, me.to_x(-1))
        elif k == 1:
            here(1, 2)
            go(1, 3, 2, me.to_x(1))
        elif k == 2:
            here(3)
            put(4, 0, 4)
            go(4, 5, 3, me.to_z(1))
            go(4, 6, 4, me.to_z(-1))
        elif k in (3, 4):
            at = 2 * k - 1
            here(at, at + 1)
            go(at, at + 2, 2 * k - 1, me.to_z(1))
            go(at + 1, at + 3, 2 * k, me.to_z(-1))
        elif k == 5:
            here(9, 10)
            go(9, 11, 9, me.to_z(1))
        elif k == 6:
            here(11)
            put(12, 4, 12)
            go(12, 13, 10, up)
            go(12, 14, 11, down)
        elif k == 7:
            here(13, 14)
            go(13, 15, 12, up)
        elif k == 8:
            here(15)
            put(16, 12, 16)
            go(16, 17, 13, sib)
        elif k == 9:
            here(17)
            put(18, 16, 18)

    def panel(group, core, s):
        if group < 2:
            return full[group * 4 + s, pl.ds(core * 16, 16)].reshape(256, ROWS)
        return full[8 + s // 2, pl.ds((s % 2) * 16 + core * 8, 8)].reshape(128, ROWS)

    def lanes(group):
        return pl.ds(*GROUPS[group])

    def power(group, slots, last):
        for out, core in enumerate((other, me.core)):
            value = acc[out, :, lanes(group)] if slots[0] else None
            for s in slots:
                one = dot(cols[s], panel(group, core, s), 1, 1)
                value = one if value is None else value + one
            if last and out == 0:
                piece = away.at[0, :, lanes(group)]
                away[0, :, lanes(group)] = value.astype(BF)
                send(piece, came.at[0, :, lanes(group)], xs.at[group], xr.at[group], sib)
            else:
                acc[out, :, lanes(group)] = value

    def spread_out(group):
        wait(came.at[0, :, lanes(group)], xr.at[group])
        spread[0, :, lanes(group)] = (acc[1, :, lanes(group)] + came[0, :, lanes(group)].astype(F32)).astype(BF)
        piece = spread.at[0, :, lanes(group)]
        send(piece, spread.at[2, :, lanes(group)], ps.at[group], pr.at[group], up)
        send(piece, spread.at[1, :, lanes(group)], ps.at[3 + group], pr.at[3 + group], down)

    def hand_on(group):
        top, low_part = pl.ds(0, half), pl.ds(half, half)
        wait(spread.at[2, :, lanes(group)], pr.at[group])
        send(spread.at[2, top, lanes(group)], spread.at[3, top, lanes(group)],
             ps.at[6 + group], pr.at[6 + group], up)
        wait(spread.at[1, :, lanes(group)], pr.at[3 + group])
        send(spread.at[1, low_part, lanes(group)], spread.at[3, low_part, lanes(group)],
             ps.at[9 + group], pr.at[9 + group], down)

    def far_here(group):
        wait(spread.at[3, pl.ds(0, half), lanes(group)], pr.at[6 + group])
        wait(spread.at[3, pl.ds(0, half), lanes(group)], pr.at[9 + group])

    def at_tick(t, tick, body, *args):
        @pl.when(t == tick)
        def _():
            body(*args)

    def forward_cols():
        wait(slot(0, 0), nr.at[1])
        send(slot(2, 0), slot(3, 0), ns.at[5], nr.at[5], up)
        wait(slot(0, 1), nr.at[2])
        send(slot(1, 1), slot(3, 1), ns.at[6], nr.at[6], down)

    def near_cols():
        wait(slot(0, 0), nr.at[3])
        wait(slot(0, 0), nr.at[4])

    def far_cols():
        wait(slot(0, 0), nr.at[5])
        wait(slot(0, 0), nr.at[6])

    done = [entry(k) + SKEW * STAGES for k in range(UNITS)]

    def tick(t, carry):
        at_tick(t, FORWARD, forward_cols)
        at_tick(t, done[4] + 2, spread_out, 0)
        at_tick(t, done[7] + 1, spread_out, 1)
        for stage in range(STAGES, -1, -1):
            turn = t - SKEW * stage
            later = turn - START
            k = jnp.where(turn < 2, turn, (later if SPACE == 1 else lax.div(later, SPACE)) + 2)
            valid = jnp.logical_and(
                jnp.logical_or(
                    jnp.logical_and(turn >= 0, turn < 2),
                    jnp.logical_and(later >= 0, lax.rem(later, SPACE) == 0 if SPACE > 1 else True),
                ),
                k < UNITS,
            )
            unit = unit_at(k)

            @pl.when(valid)
            def _():
                if stage == 0:
                    at_tick(t, entry(2), near_cols)
                    at_tick(t, entry(4), far_cols)
                    gram(unit)
                axis = me.core
                for first in (0, 1):
                    @pl.when(axis == first)
                    def _():
                        sums[first].run(stage, unit)

        for k in range(10):
            at_tick(t, SKEW * k, rider, k)
        at_tick(t, done[3], power, 0, (0, 1, 2), False)
        at_tick(t, done[4], power, 0, (3,), True)
        at_tick(t, done[6], power, 1, (0, 1, 2), False)
        at_tick(t, done[7], power, 1, (3,), True)
        at_tick(t, done[8], power, 2, (0, 1), False)
        at_tick(t, done[8], hand_on, 0)
        return carry

    lax.fori_loop(0, done[-1] + 1, tick, 0)

    power(2, (2, 3), True)

    def push(core, out, group, slots, at, length, start=False):
        value = None
        for s in slots:
            one = dot(spread[s, :, pl.ds(at, length)], panel(group, core, s)[:, at:at + length], 1, 1)
            value = one if value is None else value + one
        acc[out, :, lanes(group)] = value if start else acc[out, :, lanes(group)] + value

    for group in range(3):
        push(other, 0, group, (0,), 0, 512, True)
    spread_out(2)
    hand_on(1)
    for group in range(3):
        push(other, 0, group, (1, 2), 0, 512)
        push(me.core, 1, group, (0, 1, 2), 0, 512, True)
    hand_on(2)
    far_here(0)
    far_here(1)
    for group in range(3):
        push(other, 0, group, (3,), 0, 512)
        push(other, 0, group, (0, 1, 2), 512, 128)
        push(me.core, 1, group, (3,), 0, 512)
        push(me.core, 1, group, (0, 1, 2), 512, 128)
    far_here(2)
    for group in range(3):
        push(other, 0, group, (3,), 512, 128)
        away[1, :, lanes(group)] = acc[0, :, lanes(group)].astype(BF)
        send(away.at[1, :, lanes(group)], came.at[1, :, lanes(group)],
             xs.at[3 + group], xr.at[3 + group], sib)
    for group in range(3):
        push(me.core, 1, group, (3,), 512, 128)

    factor = 0.55 * jnp.sqrt(jnp.float32(D)) / jnp.sqrt(tot[18, 0:1, 0:1] + 1e-06)
    scale = 0.2 * max(D, FF) ** 0.5
    square = factor * factor
    for group in range(3):
        wait(came.at[1, :, lanes(group)], xr.at[3 + group])

    def finish(i, carry):
        rows = pl.ds(pl.multiple_of(i * strip, strip), strip)
        second = acc[1, rows] + came[1, rows].astype(F32)
        first = spread[0, rows].astype(F32)
        update[rows] = (
            (scale * factor)
            * (3.4445 * cols[0, rows].astype(F32) + square * (-4.775 * first + square * (2.0315 * second)))
        ).astype(BF)
        return carry

    lax.fori_loop(0, COLS // strip, finish, 0)

    for unit in range(UNITS):
        wait(got.at[pl.ds(0, 2)], ss.at[unit])
    for index in (0, 1, 3, 4, 5, 6, 9, 10):
        wait(own0, cs.at[index])
    for index in (2, 7, 8):
        wait(cot, cs.at[index])
    wait(twin, ns.at[0])
    for index in range(1, 7):
        wait(slot(0, 0), ns.at[index])
    for index in range(14):
        wait(tot.at[0], ts.at[index])
    for group in range(3):
        wait(away.at[0, :, lanes(group)], xs.at[group])
        wait(away.at[1, :, lanes(group)], xs.at[3 + group])
        for index in (0, 3):
            wait(spread.at[0, :, lanes(group)], ps.at[index + group])
        for index in (6, 9):
            wait(spread.at[0, pl.ds(0, half), lanes(group)], ps.at[index + group])


def shards(act, cot, momentum):
    vmem, anywhere = pl.BlockSpec(memory_space=pltpu.VMEM), pl.BlockSpec(memory_space=pl.ANY)
    dma = pltpu.SemaphoreType.DMA
    panel = (UNITS, NX * NZ, PIECE, ROWS)
    tile = (COLS, ROWS)
    new_momentum, update = pl.pallas_call(
        kernel,
        out_shape=(jax.ShapeDtypeStruct(tile, F32), jax.ShapeDtypeStruct(tile, BF)),
        in_specs=[anywhere, vmem, anywhere],
        out_specs=(vmem, vmem),
        scratch_shapes=[
            pltpu.VMEM((8 * TOK, ROWS), BF),
            pltpu.VMEM((8, COLS, TOK), BF),
            pltpu.VMEM((NY, *tile), BF),
            pltpu.VMEM((ROWS, COLS), BF),
            pltpu.VMEM((ROWS, COLS), BF),
            pltpu.VMEM(tile, BF),
            pltpu.VMEM(panel, BF),
            pltpu.VMEM((UNITS, 31, PIECE, ROWS), BF),
            pltpu.VMEM(panel, BF),
            pltpu.VMEM((NY, *tile), BF),
            pltpu.VMEM((2, *tile), F32),
            pltpu.VMEM((2, *tile), BF),
            pltpu.VMEM((2, *tile), BF),
            pltpu.VMEM((19, 8, 128), F32),
            dma((2,)), dma((11,)), dma((11,)), dma((7,)), dma((7,)), dma((UNITS,)), dma((UNITS, STAGES)),
            dma((12,)), dma((12,)), dma((6,)), dma((6,)), dma((14,)), dma((19,)),
        ],
        compiler_params=pltpu.CompilerParams(
            collective_id=0, has_side_effects=True, vmem_limit_bytes=53 * 2**20
        ),
        name="muon_step",
    )(act, cot.T, momentum.T)
    return (new_momentum.T, update.T)


def solution(mesh):
    in_specs = (P(None, "dp"), P("dp", "tensor"), P("dp", "tensor"))
    out_specs = (P("dp", "tensor"), P("dp", "tensor"))
    return jax.shard_map(shards, mesh=mesh, in_specs=in_specs, out_specs=out_specs, check_vma=False)
```

```python
import functools

import jax
import jax.numpy as jnp
from jax import lax
from jax.experimental import pallas as pl
from jax.experimental.pallas import tpu as pltpu
from jax.sharding import PartitionSpec as P

D = 5120
FF = 25600
NY, NX, NZ = 4, 4, 8
ROWS, COLS = 640, 800
TOK = 256
UNITS, PIECE = 10, 16
MESH = pl.DeviceIdType.MESH
BF, F32 = jnp.bfloat16, jnp.float32


class Place:
    def __init__(self):
        self.dp, self.tensor = lax.axis_index("dp"), lax.axis_index("tensor")
        self.y, self.core = self.dp // 2, self.dp % 2
        self.x, self.z = self.tensor // NZ, self.tensor % NZ

    def to_y(self, step):
        return (lax.rem(self.y + step + NY, NY) * 2 + self.core, self.tensor)

    def to_x(self, step):
        return (self.dp, lax.rem(self.x + step + NX, NX) * NZ + self.z)

    def to_z(self, step):
        return (self.dp, self.x * NZ + lax.rem(self.z + step + NZ, NZ))

    def sibling(self):
        return (self.y * 2 + 1 - self.core, self.tensor)


def send(src, dst, send_sem, recv_sem, device):
    copy = pltpu.make_async_remote_copy(
        src_ref=src, dst_ref=dst, send_sem=send_sem, recv_sem=recv_sem,
        device_id=device, device_id_type=MESH,
    )
    copy.start()


def wait(ref, sem):
    pltpu.make_async_copy(ref, ref, sem).wait()


def greet(devices):
    barrier = pltpu.get_barrier_semaphore()
    for device in devices:
        pl.semaphore_signal(barrier, inc=1, device_id=device, device_id_type=MESH)
    pl.semaphore_wait(barrier, len(devices))


def dot(a, b, ca, cb):
    return lax.dot_general(a, b, (((ca,), (cb,)), ((), ())), preferred_element_type=F32)


class Sum:
    def __init__(self, n1, n2, p1, p2, to1, to2, part, got, full, ss, rs):
        self.n1, self.n2, self.p1 = n1, n2, p1
        self.part, self.got, self.full, self.ss, self.rs = part, got, full, ss, rs
        self.h1, self.h2 = h1, h2 = n1 // 2, n2 // 2
        self.dev1 = {sign: to1(sign) for sign in (1, -1)}
        self.dev2 = {sign: to2(sign) for sign in (1, -1)}
        self.at1 = {d: lax.rem(p1 + d + n1, n1) * n2 for d in range(-h1, h1 + 1)}
        self.at2 = {d: p1 * n2 + lax.rem(p2 + d + n2, n2) for d in range(-h2, h2 + 1)}
        self.msg, offset = {}, 0
        for stage in range(2 * h1 + 2 * h2):
            for role in (0, 1):
                kind, length = self.kind(stage, role)
                if kind is not None:
                    self.msg[stage, role] = (length, offset)
                    offset += length if stage < h1 + h2 else 0

    def kind(self, stage, role):
        h1, h2, n2 = self.h1, self.h2, self.n2
        if stage < h1:
            return "rs1", n2 // 2 if stage == 0 else n2
        if stage < h1 + h2:
            return ("rs2" if stage > h1 or role == 0 else None), 1
        if stage < h1 + 2 * h2:
            last = stage == h1 + 2 * h2 - 1
            return (None if last and role == 1 else "ag2"), 1
        last = stage == 2 * h1 + 2 * h2 - 1
        return "ag1", n2 // 2 if last else n2

    def second(self, role, unit, table, d=1):
        upward = lax.rem(unit, 2) == role
        pick = lambda a, b: jnp.where(upward, a, b)
        a, b = table[d], table[-d]
        return tuple(map(pick, a, b)) if isinstance(a, tuple) else pick(a, b)

    def launch(self, stage, role, unit, src, dst):
        first = stage < self.h1 or stage >= self.h1 + 2 * self.h2
        to = self.dev1[1 - 2 * role] if first else self.second(role, unit, self.dev2)
        send(src, dst, self.ss.at[unit], self.rs.at[unit, stage], to)

    def slab(self, stage, role, unit):
        length, offset = self.msg[stage, role]
        return self.got.at[unit, pl.ds(offset, length)]

    def add(self, unit, at, length, *slabs, out=None):
        total = self.part[unit, pl.ds(at, length)].astype(F32)
        for slab in slabs:
            total = total + slab[...].astype(F32)
        if out is None:
            self.part[unit, pl.ds(at, length)] = total.astype(BF)
        else:
            out[unit, pl.ds(at, length)] = total.astype(BF)

    def settle(self, stage, unit):
        total = sum(self.msg[stage, role][0] for role in (0, 1) if (stage, role) in self.msg)
        wait(self.part.at[unit, pl.ds(0, total)], self.rs.at[unit, stage])

    def run(self, stage, unit):
        h1, h2, n2 = self.h1, self.h2, self.n2
        part, full = self.part, self.full
        if stage > 0:
            self.settle(stage - 1, unit)
        if stage < h1:
            step = h1 - stage
            for role in (0, 1):
                sign = 1 - 2 * role
                if stage == 0:
                    at = self.at1[h1] + role * (n2 // 2)
                else:
                    at = self.at1[sign * step]
                    if stage == 1:
                        self.add(unit, at + role * (n2 // 2), n2 // 2, self.slab(0, role, unit))
                    else:
                        self.add(unit, at, n2, self.slab(stage - 1, role, unit))
                length = self.msg[stage, role][0]
                self.launch(stage, role, unit, part.at[unit, pl.ds(at, length)],
                            self.slab(stage, role, unit))
        elif stage < h1 + h2:
            if stage == h1:
                own = self.p1 * n2
                self.add(unit, own, n2, self.slab(stage - 1, 0, unit), self.slab(stage - 1, 1, unit))
            step = h1 + h2 - stage
            for role in (0, 1):
                if (stage, role) not in self.msg:
                    continue
                at = self.second(role, unit, self.at2, step)
                if stage > h1 and (stage - 1, role) in self.msg:
                    self.add(unit, at, 1, self.slab(stage - 1, role, unit))
                self.launch(stage, role, unit, part.at[unit, pl.ds(at, 1)],
                            self.slab(stage, role, unit))
        elif stage < h1 + 2 * h2:
            at = self.at2[0]
            hop = stage - h1 - h2
            if hop == 0:
                self.add(unit, at, 1, self.slab(stage - 1, 0, unit), self.slab(stage - 1, 1, unit),
                         out=full)
            for role in (0, 1):
                if (stage, role) in self.msg:
                    at = self.second(1 - role, unit, self.at2, hop)
                    piece = full.at[unit, pl.ds(at, 1)]
                    self.launch(stage, role, unit, piece, piece)
        elif stage < 2 * h1 + 2 * h2:
            hop = stage - h1 - 2 * h2
            for role in (0, 1):
                sign = 1 - 2 * role
                at = self.at1[-sign * hop]
                length = self.msg[stage, role][0]
                if length < n2:
                    at = at + role * (n2 // 2)
                piece = full.at[unit, pl.ds(at, length)]
                self.launch(stage, role, unit, piece, piece)


STAGES = 12
SKEW = 3
SPACE = 2
START = 18
FORWARD = 10
GROUPS = ((0, 256), (256, 256), (512, 128))


def unit_at(k):
    return jnp.where(k == 1, 4, jnp.where(jnp.logical_and(k >= 2, k < 5), k - 1, jnp.where(k == 0, 0, k)))


def entry(k):
    return k if k < 2 else START + SPACE * (k - 2)


def kernel(act_hbm, cot_hbm, mom_hbm, newm_hbm, update, act, newm, held, cols, ours, theirs, twin,
           part, got, full, spread, acc, away, came, tot,
           ls, cs, cr, ns, nr, ss, rs, ps, pr, xs, xr, ts, tr):
    me = Place()
    up, down, sib = me.to_y(1), me.to_y(-1), me.sibling()
    load_act = pltpu.make_async_copy(act_hbm, act, ls.at[0])
    load_mom = pltpu.make_async_copy(mom_hbm, newm, ls.at[1])
    cot = held.at[me.dp]
    load_cot = pltpu.make_async_copy(cot_hbm, cot, ls.at[2])
    load_cot.start()
    load_act.start()
    load_mom.start()
    greet([up, down, sib, me.to_x(1), me.to_x(-1), me.to_z(1), me.to_z(-1)])

    load_cot.wait()

    half = COLS // 2
    other = 1 - me.core

    def block(step, core):
        return lax.rem(me.y + step + NY, NY) * 2 + core

    def bit(step, core, h):
        return held.at[block(step, core), pl.ds(h * half, half)]

    own0, own1 = cot.at[pl.ds(0, half)], cot.at[pl.ds(half, half)]
    send(own0, bit(0, me.core, 0), cs.at[0], cr.at[0], up)
    send(own1, bit(0, me.core, 1), cs.at[1], cr.at[1], down)
    send(cot, held.at[me.dp], cs.at[2], cr.at[2], sib)
    send(own1, bit(0, me.core, 1), cs.at[3], cr.at[3], up)
    send(own0, bit(0, me.core, 0), cs.at[4], cr.at[4], down)
    load_act.wait()

    def term(tokens, rows):
        return dot(rows, act[pl.ds(pl.multiple_of(tokens * TOK, TOK), TOK), :], 1, 0)

    acc[0] = term(me.dp, cot[...])
    wait(own0, cr.at[0])
    send(bit(-1, me.core, 0), bit(-1, me.core, 0), cs.at[5], cr.at[5], up)
    wait(own1, cr.at[1])
    send(bit(1, me.core, 1), bit(1, me.core, 1), cs.at[6], cr.at[6], down)
    wait(cot, cr.at[2])
    acc[0] += term(block(0, other), held[block(0, other)])
    low, high = held.at[block(-1, me.core)], held.at[block(1, me.core)]
    wait(own1, cr.at[3])
    send(low, low, cs.at[7], cr.at[7], sib)
    wait(own0, cr.at[4])
    send(high, high, cs.at[8], cr.at[8], sib)
    acc[0] += term(block(-1, me.core), low[...])
    acc[0] += term(block(1, me.core), high[...])
    wait(low, cr.at[7])
    acc[0] += term(block(-1, other), held[block(-1, other)])
    wait(high, cr.at[8])
    acc[0] += term(block(1, other), held[block(1, other)])
    wait(own0, cr.at[5])
    send(bit(2, me.core, 0), bit(2, me.core, 0), cs.at[9], cr.at[9], sib)
    wait(own1, cr.at[6])
    send(bit(2, me.core, 1), bit(2, me.core, 1), cs.at[10], cr.at[10], sib)
    acc[0] += term(block(2, me.core), held[block(2, me.core)])
    wait(own0, cr.at[9])
    wait(own1, cr.at[10])
    acc[0] += term(block(2, other), held[block(2, other)])
    load_mom.wait()

    strip = 80

    def momentum(i, squares):
        rows = pl.ds(pl.multiple_of(i * strip, strip), strip)
        grad = acc[0, rows]
        updated = 0.95 * newm[rows] + grad
        newm[rows] = updated
        value = grad + 0.95 * updated
        cols[0, rows] = value.astype(BF)
        return squares + jnp.sum(value * value, axis=0, keepdims=True)

    squares = lax.fori_loop(0, COLS // strip, momentum, jnp.zeros((1, ROWS), F32))
    store_mom = pltpu.make_async_copy(newm, newm_hbm, ls.at[1])
    store_mom.start()
    tot[0] = jnp.full((8, 128), jnp.sum(squares), F32)

    def slot(s, h):
        return cols.at[s, pl.ds(h * half, half)]

    send(cols.at[0], twin, ns.at[0], nr.at[0], sib)
    send(slot(0, 0), slot(2, 0), ns.at[1], nr.at[1], up)
    send(slot(0, 1), slot(1, 1), ns.at[2], nr.at[2], down)
    send(slot(0, 1), slot(2, 1), ns.at[3], nr.at[3], up)
    send(slot(0, 0), slot(1, 0), ns.at[4], nr.at[4], down)
    ours[...] = cols[0].T
    wait(twin, nr.at[0])
    theirs[...] = twin[...].T

    sums = (
        Sum(NX, NZ, me.x, me.z, me.to_x, me.to_z, part, got, full, ss, rs),
        Sum(NZ, NX, me.z, me.x, me.to_z, me.to_x, part, got, full, ss, rs),
    )

    def gram(unit):
        def put(at, chip_rows, length, s):
            value = dot(chip_rows, cols[s], 1, 0).astype(BF)
            part[unit, pl.ds(at, length // PIECE)] = value.reshape(length // PIECE, PIECE, ROWS)

        def from_cores(at0, at1, first, length, s):
            put(jnp.where(me.core == 0, at0, at1), ours[pl.ds(first, length), :], length, s)
            put(jnp.where(me.core == 0, at1, at0), theirs[pl.ds(first, length), :], length, s)

        @pl.when(unit < 8)
        def _():
            first = pl.multiple_of((unit // 4) * 256, 256)
            from_cores(0, 16, first, 256, lax.rem(unit, 4))

        @pl.when(unit >= 8)
        def _():
            for k in (0, 1):
                from_cores(16 * k, 16 * k + 8, 512, 128, (unit - 8) * 2 + k)

    def rider(k):
        def go(src, dst, index, device):
            send(tot.at[src], tot.at[dst], ts.at[index], tr.at[dst], device)

        def here(*slots):
            for s in slots:
                wait(tot.at[s], tr.at[s])

        def put(dst, first, last):
            value = tot[first]
            for s in range(first + 1, last):
                value = value + tot[s]
            tot[dst] = value

        if k == 0:
            go(0, 1, 0, me.to_x(1))
            go(0, 2, 1, me.to_x(-1))
        elif k == 1:
            here(1, 2)
            go(1, 3, 2, me.to_x(1))
        elif k == 2:
            here(3)
            put(4, 0, 4)
            go(4, 5, 3, me.to_z(1))
            go(4, 6, 4, me.to_z(-1))
        elif k in (3, 4):
            at = 2 * k - 1
            here(at, at + 1)
            go(at, at + 2, 2 * k - 1, me.to_z(1))
            go(at + 1, at + 3, 2 * k, me.to_z(-1))
        elif k == 5:
            here(9, 10)
            go(9, 11, 9, me.to_z(1))
        elif k == 6:
            here(11)
            put(12, 4, 12)
            go(12, 13, 10, up)
            go(12, 14, 11, down)
        elif k == 7:
            here(13, 14)
            go(13, 15, 12, up)
        elif k == 8:
            here(15)
            put(16, 12, 16)
            go(16, 17, 13, sib)
        elif k == 9:
            here(17)
            put(18, 16, 18)

    def panel(group, core, s):
        if group < 2:
            return full[group * 4 + s, pl.ds(core * 16, 16)].reshape(256, ROWS)
        return full[8 + s // 2, pl.ds((s % 2) * 16 + core * 8, 8)].reshape(128, ROWS)

    def lanes(group):
        return pl.ds(*GROUPS[group])

    def power(group, slots, last):
        for out, core in enumerate((other, me.core)):
            value = acc[out, :, lanes(group)] if slots[0] else None
            for s in slots:
                one = dot(cols[s], panel(group, core, s), 1, 1)
                value = one if value is None else value + one
            if last and out == 0:
                piece = away.at[0, :, lanes(group)]
                away[0, :, lanes(group)] = value.astype(BF)
                send(piece, came.at[0, :, lanes(group)], xs.at[group], xr.at[group], sib)
            else:
                acc[out, :, lanes(group)] = value

    def spread_out(group):
        wait(came.at[0, :, lanes(group)], xr.at[group])
        spread[0, :, lanes(group)] = (acc[1, :, lanes(group)] + came[0, :, lanes(group)].astype(F32)).astype(BF)
        piece = spread.at[0, :, lanes(group)]
        send(piece, spread.at[2, :, lanes(group)], ps.at[group], pr.at[group], up)
        send(piece, spread.at[1, :, lanes(group)], ps.at[3 + group], pr.at[3 + group], down)

    def hand_on(group):
        top, low_part = pl.ds(0, half), pl.ds(half, half)
        wait(spread.at[2, :, lanes(group)], pr.at[group])
        send(spread.at[2, top, lanes(group)], spread.at[3, top, lanes(group)],
             ps.at[6 + group], pr.at[6 + group], up)
        wait(spread.at[1, :, lanes(group)], pr.at[3 + group])
        send(spread.at[1, low_part, lanes(group)], spread.at[3, low_part, lanes(group)],
             ps.at[9 + group], pr.at[9 + group], down)

    def far_here(group):
        wait(spread.at[3, pl.ds(0, half), lanes(group)], pr.at[6 + group])
        wait(spread.at[3, pl.ds(0, half), lanes(group)], pr.at[9 + group])

    def at_tick(t, tick, body, *args):
        @pl.when(t == tick)
        def _():
            body(*args)

    def forward_cols():
        wait(slot(0, 0), nr.at[1])
        send(slot(2, 0), slot(3, 0), ns.at[5], nr.at[5], up)
        wait(slot(0, 1), nr.at[2])
        send(slot(1, 1), slot(3, 1), ns.at[6], nr.at[6], down)

    def near_cols():
        wait(slot(0, 0), nr.at[3])
        wait(slot(0, 0), nr.at[4])

    def far_cols():
        wait(slot(0, 0), nr.at[5])
        wait(slot(0, 0), nr.at[6])

    done = [entry(k) + SKEW * STAGES for k in range(UNITS)]

    def tick(t, carry):
        at_tick(t, FORWARD, forward_cols)
        at_tick(t, done[4] + 2, spread_out, 0)
        at_tick(t, done[7] + 1, spread_out, 1)
        for stage in range(STAGES, -1, -1):
            turn = t - SKEW * stage
            later = turn - START
            k = jnp.where(turn < 2, turn, (later if SPACE == 1 else lax.div(later, SPACE)) + 2)
            valid = jnp.logical_and(
                jnp.logical_or(
                    jnp.logical_and(turn >= 0, turn < 2),
                    jnp.logical_and(later >= 0, lax.rem(later, SPACE) == 0 if SPACE > 1 else True),
                ),
                k < UNITS,
            )
            unit = unit_at(k)

            @pl.when(valid)
            def _():
                if stage == 0:
                    at_tick(t, entry(2), near_cols)
                    at_tick(t, entry(4), far_cols)
                    gram(unit)
                axis = me.core
                for first in (0, 1):
                    @pl.when(axis == first)
                    def _():
                        sums[first].run(stage, unit)

        for k in range(10):
            at_tick(t, SKEW * k, rider, k)
        at_tick(t, done[3], power, 0, (0, 1, 2), False)
        at_tick(t, done[4], power, 0, (3,), True)
        at_tick(t, done[6], power, 1, (0, 1, 2), False)
        at_tick(t, done[7], power, 1, (3,), True)
        at_tick(t, done[8], power, 2, (0, 1), False)
        at_tick(t, done[8], hand_on, 0)
        return carry

    lax.fori_loop(0, done[-1] + 1, tick, 0)

    power(2, (2, 3), True)

    def push(core, out, group, slots, at, length, start=False):
        value = None
        for s in slots:
            one = dot(spread[s, :, pl.ds(at, length)], panel(group, core, s)[:, at:at + length], 1, 1)
            value = one if value is None else value + one
        acc[out, :, lanes(group)] = value if start else acc[out, :, lanes(group)] + value

    for group in range(3):
        push(other, 0, group, (0,), 0, 512, True)
    spread_out(2)
    hand_on(1)
    for group in range(3):
        push(other, 0, group, (1, 2), 0, 512)
        push(me.core, 1, group, (0, 1, 2), 0, 512, True)
    hand_on(2)
    far_here(0)
    far_here(1)
    for group in range(3):
        push(other, 0, group, (3,), 0, 512)
        push(other, 0, group, (0, 1, 2), 512, 128)
        push(me.core, 1, group, (3,), 0, 512)
        push(me.core, 1, group, (0, 1, 2), 512, 128)
    far_here(2)
    for group in range(3):
        push(other, 0, group, (3,), 512, 128)
        away[1, :, lanes(group)] = acc[0, :, lanes(group)].astype(BF)
        send(away.at[1, :, lanes(group)], came.at[1, :, lanes(group)],
             xs.at[3 + group], xr.at[3 + group], sib)
    for group in range(3):
        push(me.core, 1, group, (3,), 512, 128)

    factor = 0.55 * jnp.sqrt(jnp.float32(D)) / jnp.sqrt(tot[18, 0:1, 0:1] + 1e-06)
    scale = 0.2 * max(D, FF) ** 0.5
    square = factor * factor
    for group in range(3):
        wait(came.at[1, :, lanes(group)], xr.at[3 + group])

    def finish(i, carry):
        rows = pl.ds(pl.multiple_of(i * strip, strip), strip)
        second = acc[1, rows] + came[1, rows].astype(F32)
        first = spread[0, rows].astype(F32)
        update[rows] = (
            (scale * factor)
            * (3.4445 * cols[0, rows].astype(F32) + square * (-4.775 * first + square * (2.0315 * second)))
        ).astype(BF)
        return carry

    lax.fori_loop(0, COLS // strip, finish, 0)

    store_mom.wait()
    for unit in range(UNITS):
        wait(got.at[pl.ds(0, 2)], ss.at[unit])
    for index in (0, 1, 3, 4, 5, 6, 9, 10):
        wait(own0, cs.at[index])
    for index in (2, 7, 8):
        wait(cot, cs.at[index])
    wait(twin, ns.at[0])
    for index in range(1, 7):
        wait(slot(0, 0), ns.at[index])
    for index in range(14):
        wait(tot.at[0], ts.at[index])
    for group in range(3):
        wait(away.at[0, :, lanes(group)], xs.at[group])
        wait(away.at[1, :, lanes(group)], xs.at[3 + group])
        for index in (0, 3):
            wait(spread.at[0, :, lanes(group)], ps.at[index + group])
        for index in (6, 9):
            wait(spread.at[0, pl.ds(0, half), lanes(group)], ps.at[index + group])


def shards(act, cot, momentum):
    vmem, anywhere = pl.BlockSpec(memory_space=pltpu.VMEM), pl.BlockSpec(memory_space=pl.ANY)
    dma = pltpu.SemaphoreType.DMA
    panel = (UNITS, NX * NZ, PIECE, ROWS)
    tile = (COLS, ROWS)
    new_momentum, update = pl.pallas_call(
        kernel,
        out_shape=(jax.ShapeDtypeStruct(tile, F32), jax.ShapeDtypeStruct(tile, BF)),
        in_specs=[anywhere, anywhere, anywhere],
        out_specs=(anywhere, vmem),
        scratch_shapes=[
            pltpu.VMEM((8 * TOK, ROWS), BF),
            pltpu.VMEM(tile, F32),
            pltpu.VMEM((8, COLS, TOK), BF),
            pltpu.VMEM((NY, *tile), BF),
            pltpu.VMEM((ROWS, COLS), BF),
            pltpu.VMEM((ROWS, COLS), BF),
            pltpu.VMEM(tile, BF),
            pltpu.VMEM(panel, BF),
            pltpu.VMEM((UNITS, 31, PIECE, ROWS), BF),
            pltpu.VMEM(panel, BF),
            pltpu.VMEM((NY, *tile), BF),
            pltpu.VMEM((2, *tile), F32),
            pltpu.VMEM((2, *tile), BF),
            pltpu.VMEM((2, *tile), BF),
            pltpu.VMEM((19, 8, 128), F32),
            dma((3,)), dma((11,)), dma((11,)), dma((7,)), dma((7,)), dma((UNITS,)), dma((UNITS, STAGES)),
            dma((12,)), dma((12,)), dma((6,)), dma((6,)), dma((14,)), dma((19,)),
        ],
        compiler_params=pltpu.CompilerParams(
            collective_id=0, has_side_effects=True, vmem_limit_bytes=61 * 2**20
        ),
        name="muon_step",
    )(act, cot.T, momentum.T)
    return (new_momentum.T, update.T)


def solution(mesh):
    in_specs = (P(None, "dp"), P("dp", "tensor"), P("dp", "tensor"))
    out_specs = (P("dp", "tensor"), P("dp", "tensor"))
    return jax.shard_map(shards, mesh=mesh, in_specs=in_specs, out_specs=out_specs, check_vma=False)
```
